32 devices in a mesh: dp: 4 (over y, x), ctx: 4 (over z), mp: 2 (over core).
Axes of the slice: x: 2, y: 2, z: 4, core: 2. Of those that a mesh axis runs over, the one named last changes fastest.
Arguments:
- tokens: bfloat16 [4, 512, 4096], P('dp', 'ctx'), may hold values from -52 to 52
- x_weight: bfloat16 [4096, 8192], P(('dp', 'ctx'), 'mp'), may hold values from -0.09375 to 0.09375
- bc_weight: bfloat16 [4096, 1024], P(('dp', 'ctx'), 'mp'), may hold values from -0.09375 to 0.09375
- dt_weight: bfloat16 [4096, 128], P(('dp', 'ctx'), 'mp'), may hold values from -0.0234375 to 0.0234375
- conv_x: float32 [5, 8192], P(None, 'mp'), may hold values from -0.5 to 0.5
- conv_bc: float32 [5, 1024], P(None, 'mp'), may hold values from -0.5 to 0.5
- dt_bias: float32 [128], P('mp'), may hold values from -4.5 to -2.5
- a_log: float32 [128], P('mp')
- d_skip: float32 [128], P('mp'), may hold values from 0.5 to 1.5
- norm_gain: float32 [8192], P('mp'), may hold values from 0.5 to 1.5
Outputs:
- mixer_out: bfloat16 [4, 512, 8192], P('dp', 'ctx', 'mp')
- kurtosis: float32 [4096], P('mp')
The draws below stay inside these ranges and needn't reach their ends.
All inputs are finite; a program needn't handle non-finite values.
Results may differ from the reference program's by a relative error of at most 0.015.
Values may be sent and summed in bfloat16 or wider, within the bound.
A program may use at most 128 MiB of HBM per device.

```python
import jax
import jax.numpy as jnp
from jax import lax

D = 4096
ROOT = 64
HEADS = 128
P_SIZE = 64
G = 4
NS = 128
KW = 4
TOK_DEV = 128
SEQLEN = 512
BATCH = 4
INNER = 8192
BCW = 1024
N_CTX = 4


def draw_tokens(key, part):
    sample_key, row_key, col_key = jax.random.split(jax.random.fold_in(key, 11), 3)
    full_shape = (BATCH, SEQLEN, D)
    samples = jnp.clip(jax.random.normal(sample_key, full_shape, jnp.float32), -6.0, 6.0)
    row_scale = jnp.exp(jax.random.uniform(row_key, (BATCH, SEQLEN, 1), jnp.float32) * jnp.log(10.0))
    position = (jnp.arange(BATCH, dtype=jnp.float32)[:, None, None] * SEQLEN + jnp.arange(SEQLEN, dtype=jnp.float32)[None, :, None]) / (BATCH * SEQLEN)
    trend = jnp.exp(0.5 * jnp.log(3.0) * position)
    col_scale = jnp.exp(jax.random.uniform(col_key, (D,), jnp.float32) * jnp.log(10.0))
    return (0.05 * samples * row_scale * trend * col_scale).astype(jnp.bfloat16)


def draw_a_log(key, part):
    pick_key, level_key = jax.random.split(jax.random.fold_in(key, 23), 2)
    pick = jax.random.uniform(pick_key, (HEADS,), jnp.float32)
    level = jax.random.uniform(level_key, (HEADS,), jnp.float32)
    slow_share = 0.55
    slow_low = jnp.log(0.5 / SEQLEN)
    slow_value = slow_low + level * jnp.log(60.0)
    fast_low = jnp.log(30.0 / SEQLEN)
    fast_value = fast_low + level * (0.0 - fast_low)
    return jnp.where(pick < slow_share, slow_value, fast_value).astype(jnp.float32)


def steps_of(own_key, dims, cuts, least, top_value):
    def one(dim, blocks):
        heights = jax.random.uniform(jax.random.fold_in(jax.random.fold_in(own_key, 6), dim), (blocks,), jnp.float32, least / len(cuts), top_value / len(cuts))
        return jnp.repeat(jnp.exp(heights), dims[dim] // blocks).reshape((-1,) + (1,) * (len(dims) - dim - 1))

    gain = one(*cuts[0])
    for cut in cuts[1:]:
        gain = gain * one(*cut)
    return gain


def bell_draw(stream_key, dims, scale, bound, cuts=(), kind=jnp.bfloat16):
    array = scale * jax.random.normal(stream_key, dims, jnp.float32)
    if cuts:
        array = array * steps_of(stream_key, dims, cuts, -0.22, 0.18)
    return jnp.clip(array, -bound, bound).astype(kind)


def setup_inputs(seed: int = 0) -> dict:
    seeds = jax.random.split(jax.random.key(seed), 11)
    tokens = draw_tokens(jax.random.fold_in(seeds[10], 71), 0)
    x_weight = bell_draw(seeds[1], (D, INNER), D ** -0.5, 0.09375, ((0, 16), (1, 2)))
    bc_weight = bell_draw(seeds[2], (D, BCW), D ** -0.5, 0.09375, ((0, 16), (1, 2)))
    dt_weight = bell_draw(seeds[3], (D, HEADS), (16 * D) ** -0.5, 0.0234375, ((0, 16), (1, 2)))
    conv_x = jnp.clip(jax.random.uniform(seeds[4], (KW + 1, INNER), jnp.float32, -0.5, 0.5) * steps_of(seeds[4], (KW + 1, INNER), ((1, 2),), -0.4, 0.0), -0.5, 0.5)
    conv_bc = jnp.clip(jax.random.uniform(seeds[5], (KW + 1, BCW), jnp.float32, -0.5, 0.5) * steps_of(seeds[5], (KW + 1, BCW), ((1, 2),), -0.4, 0.0), -0.5, 0.5)
    dt_bias = jnp.clip(-4.5 + 2.0 * jax.random.uniform(seeds[6], (HEADS,), jnp.float32) ** steps_of(seeds[6], (HEADS,), ((0, 2),), -0.2, 0.2), -4.5, -2.5)
    a_log = draw_a_log(jax.random.fold_in(seeds[10], 71), 0)
    d_skip = jnp.clip(0.5 + 1.0 * jax.random.uniform(seeds[8], (HEADS,), jnp.float32) ** steps_of(seeds[8], (HEADS,), ((0, 2),), -0.2, 0.2), 0.5, 1.5)
    norm_gain = jnp.clip(1.0 + 0.1 * jax.random.normal(seeds[9], (INNER,), jnp.float32), 0.5, 1.5)
    return dict(tokens=tokens, x_weight=x_weight, bc_weight=bc_weight, dt_weight=dt_weight, conv_x=conv_x, conv_bc=conv_bc, dt_bias=dt_bias, a_log=a_log, d_skip=d_skip, norm_gain=norm_gain)


HIGH = lax.Precision.HIGHEST

def hadamard_signs(sign_order):
    row_index = lax.broadcasted_iota(jnp.int32, (sign_order, sign_order), 0)
    col_index = lax.broadcasted_iota(jnp.int32, (sign_order, sign_order), 1)
    common = jnp.bitwise_and(row_index, col_index)
    parity = jnp.zeros((sign_order, sign_order), jnp.int32)
    for bit_index in range(sign_order.bit_length() - 1):
        parity = parity + jnp.bitwise_and(jnp.right_shift(common, bit_index), 1)
    return 1.0 - 2.0 * jnp.bitwise_and(parity, 1).astype(jnp.float32)

def kurtosis_from(powers, row_count):
    average = powers[0] / row_count
    second = powers[1] / row_count - average * average
    fourth = powers[3] / row_count - 4.0 * average * powers[2] / row_count + 6.0 * average * average * powers[1] / row_count - 3.0 * average * average * average * average
    return fourth / (second * second + 1e-06)

def reference(tokens, x_weight, bc_weight, dt_weight, conv_x, conv_bc, dt_bias, a_log, d_skip, norm_gain):
    row_total = BATCH * SEQLEN
    signs = hadamard_signs(ROOT)
    flattened = tokens.reshape(row_total, ROOT, ROOT).astype(jnp.float32)
    first_pass = jnp.einsum('tab,ac->tcb', flattened, signs, precision=HIGH)
    second = jnp.einsum('tcb,bd->tcd', first_pass, signs, precision=HIGH)
    rotated = (second.reshape(row_total, D) / ROOT).astype(jnp.bfloat16)
    widened = rotated.astype(jnp.float32)
    square = widened * widened
    powers = jnp.stack([lax.optimization_barrier(jnp.sum(widened, 0)), lax.optimization_barrier(jnp.sum(square, 0)), lax.optimization_barrier(jnp.sum(square * widened, 0)), lax.optimization_barrier(jnp.sum(square * square, 0))])
    kurtosis = kurtosis_from(powers, float(row_total))
    x_proj = jnp.dot(rotated, x_weight, preferred_element_type=jnp.float32).astype(jnp.bfloat16)
    bc_proj = jnp.dot(rotated, bc_weight, preferred_element_type=jnp.float32).astype(jnp.bfloat16)
    dt_proj = lax.optimization_barrier(jnp.dot(rotated, dt_weight, preferred_element_type=jnp.float32).astype(jnp.bfloat16))
    conv_taps = jnp.concatenate([conv_x, conv_bc], 1)
    per_group = HEADS // G
    block_len = TOK_DEV
    causal = lax.broadcasted_iota(jnp.int32, (block_len, block_len), 0) >= lax.broadcasted_iota(jnp.int32, (block_len, block_len), 1)

    def one_block(state_now, blk):
        x_blk, bc_blk, dt_blk = blk
        step_size = jax.nn.softplus(dt_blk.astype(jnp.float32) + dt_bias)
        decay_rate = step_size * jnp.exp(a_log)
        cumulative = jnp.cumsum(decay_rate, 0)
        block_end = cumulative[-1]
        x_heads = x_blk.reshape(block_len, G, per_group, P_SIZE).astype(jnp.float32)
        write_all = bc_blk[:, :G * NS].reshape(block_len, G, NS).astype(jnp.float32)
        read_all = bc_blk[:, G * NS:].reshape(block_len, G, NS).astype(jnp.float32)
        spread = cumulative.T[:, :, None] - cumulative.T[:, None, :]
        decay_mask = jnp.where(causal, jnp.exp(-jnp.where(causal, spread, 0.0)), 0.0)
        scores = jnp.einsum('tgn,sgn->gts', read_all, write_all, precision=HIGH)
        weights = (scores[:, None] * decay_mask.reshape(G, per_group, block_len, block_len) * step_size.T.reshape(G, per_group, 1, block_len)).astype(jnp.bfloat16)
        within_block = jnp.einsum('ghts,sghp->tghp', weights.astype(jnp.float32), x_heads, precision=HIGH)
        from_before = jnp.exp(-cumulative).reshape(block_len, G, per_group)[..., None] * jnp.einsum('tgn,ghpn->tghp', read_all, state_now, precision=HIGH)
        output_raw = within_block + from_before + d_skip.reshape(G, per_group)[None, :, :, None] * x_heads
        update = ((jnp.exp(-(block_end - cumulative)) * step_size).reshape(block_len, G, per_group)[..., None] * x_heads).astype(jnp.bfloat16)
        contrib = jnp.einsum('sghp,sgn->ghpn', update.astype(jnp.float32), write_all, precision=HIGH)
        new_state = jnp.exp(-block_end).reshape(G, per_group)[:, :, None, None] * state_now + contrib
        mean_square = lax.optimization_barrier(jnp.mean(output_raw * output_raw, -1, keepdims=True))
        normed = output_raw * lax.rsqrt(mean_square + 1e-05) * norm_gain.reshape(G, per_group, P_SIZE)
        return (new_state, normed.reshape(block_len, INNER).astype(jnp.bfloat16))

    def one_sequence(inputs):
        x_seq, bc_seq, dt_seq = inputs
        joined = jnp.concatenate([x_seq, bc_seq], 1)
        padded = jnp.pad(joined, ((KW - 1, 0), (0, 0)))
        conv_sum = conv_taps[KW]
        for tap_index in range(KW):
            conv_sum = conv_sum + conv_taps[tap_index] * padded[tap_index:tap_index + SEQLEN]
        convolved = jax.nn.silu(conv_sum).astype(jnp.bfloat16)
        blocks_x = convolved[:, :INNER].reshape(N_CTX, block_len, INNER)
        blocks_bc = convolved[:, INNER:].reshape(N_CTX, block_len, BCW)
        blocks_dt = dt_seq.reshape(N_CTX, block_len, HEADS)
        start_state = jnp.zeros((G, per_group, P_SIZE, NS), jnp.float32)
        last_state, outputs = lax.scan(one_block, start_state, (blocks_x, blocks_bc, blocks_dt))
        return outputs.reshape(SEQLEN, INNER)
    mixer_out = lax.map(one_sequence, (x_proj.reshape(BATCH, SEQLEN, INNER), bc_proj.reshape(BATCH, SEQLEN, BCW), dt_proj.reshape(BATCH, SEQLEN, HEADS)))
    return (mixer_out, kurtosis)
```

```python
import jax
import jax.numpy as jnp
from jax import lax
from jax.sharding import PartitionSpec as P

ROOT = 64
HEADS = 128
G = 4
NS = 128


HIGH = lax.Precision.HIGHEST


def passed_along(value, axis, steps):
    count = lax.axis_size(axis)
    first, last = (max(0, -steps), min(count, count - steps))
    return lax.ppermute(value, axis, [(source, source + steps) for source in range(first, last)])


def entering(array, axis, combine, identity):
    length, place = (lax.axis_size(axis), lax.axis_index(axis))
    everything = jax.tree.map(
        lambda part, kind: lax.all_gather(part.astype(kind), axis),
        array,
        (jnp.bfloat16, jnp.bfloat16),
    )
    start = jax.tree.map(
        lambda part, zero: jnp.broadcast_to(jnp.asarray(zero, part.dtype), part.shape),
        array,
        identity,
    )

    def step(k, before):
        reached = k < place
        new = combine(
            before, jax.tree.map(lambda part, own: part[k].astype(own.dtype), everything, array)
        )
        return jax.tree.map(lambda a, b: jnp.where(reached, a, b), new, before)

    return lax.fori_loop(0, length, step, start)


def hadamard_signs(sign_order):
    row_index = lax.broadcasted_iota(jnp.int32, (sign_order, sign_order), 0)
    col_index = lax.broadcasted_iota(jnp.int32, (sign_order, sign_order), 1)
    common = jnp.bitwise_and(row_index, col_index)
    parity = jnp.zeros((sign_order, sign_order), jnp.int32)
    for bit_index in range(sign_order.bit_length() - 1):
        parity = parity + jnp.bitwise_and(jnp.right_shift(common, bit_index), 1)
    return 1.0 - 2.0 * jnp.bitwise_and(parity, 1).astype(jnp.float32)


def kurtosis_from(powers, row_count):
    average = powers[0] / row_count
    second = powers[1] / row_count - average * average
    fourth = (
        powers[3] / row_count
        - 4.0 * average * powers[2] / row_count
        + 6.0 * average * average * powers[1] / row_count
        - 3.0 * average * average * average * average
    )
    return fourth / (second * second + 1e-06)


def chain_states(earlier, later):
    return (earlier[0] * later[0], later[0][:, :, None, None] * earlier[1] + later[1])


def shards_by_rows(
    tokens, x_weight, bc_weight, dt_weight, conv_x, conv_bc, dt_bias, a_log, d_skip, norm_gain
):
    tok_rows = tokens.shape[1]
    model_width = tokens.shape[2]
    signs = hadamard_signs(ROOT)
    blocks = tokens.reshape(tok_rows, ROOT, ROOT)
    first_pass = jnp.einsum(
        "tab,ac->tcb", blocks, signs.astype(jnp.bfloat16), preferred_element_type=jnp.float32
    )
    second = jnp.einsum("tcb,bd->tcd", first_pass, signs, precision=HIGH)
    rotated = (second.reshape(tok_rows, model_width) / ROOT).astype(jnp.bfloat16)
    channel_share = model_width // lax.axis_size("mp")
    own_cols = lax.dynamic_slice_in_dim(
        rotated, lax.axis_index("mp") * channel_share, channel_share, 1
    ).astype(jnp.float32)
    square = own_cols * own_cols
    powers = jnp.stack(
        [
            jnp.sum(own_cols, 0),
            jnp.sum(square, 0),
            jnp.sum(square * own_cols, 0),
            jnp.sum(square * square, 0),
        ]
    )
    row_count = float(tok_rows * lax.axis_size("dp") * lax.axis_size("ctx"))
    totals = lax.psum(powers, ("dp", "ctx"))
    kurtosis = kurtosis_from(totals, row_count)
    panels = (
        lax.all_gather(x_weight, ("dp", "ctx"), axis=0, tiled=True),
        lax.all_gather(bc_weight, ("dp", "ctx"), axis=0, tiled=True),
        lax.all_gather(dt_weight, ("dp", "ctx"), axis=0, tiled=True),
    )
    projected = tuple(
        (jnp.dot(rotated, panel, preferred_element_type=jnp.float32) for panel in panels)
    )
    x_cols = x_weight.shape[1]
    joined = jnp.concatenate(
        [projected[0].astype(jnp.bfloat16), projected[1].astype(jnp.bfloat16)], 1
    )
    dt_proj = lax.optimization_barrier(projected[2].astype(jnp.bfloat16))
    conv_taps = jnp.concatenate([conv_x, conv_bc], 1)
    kernel = conv_taps.shape[0] - 1
    rim_rows = passed_along(joined[tok_rows - (kernel - 1) :], "ctx", 1)
    padded = jnp.concatenate([rim_rows, joined], 0)
    conv_sum = conv_taps[kernel]
    for tap_index in range(kernel):
        conv_sum = conv_sum + conv_taps[tap_index] * padded[tap_index : tap_index + tok_rows]
    convolved = jax.nn.silu(conv_sum).astype(jnp.bfloat16)
    x_conv = convolved[:, :x_cols]
    group_all = lax.all_gather(convolved[:, x_cols:], "mp", axis=1, tiled=True)
    heads_dev = dt_weight.shape[1]
    head_size = x_cols // heads_dev
    per_group = HEADS // G
    groups_here = max(1, heads_dev // per_group)
    heads_local = heads_dev // groups_here
    first_group = lax.axis_index("mp") * heads_dev // per_group
    write_all = group_all[:, : G * NS].reshape(tok_rows, G, NS)
    read_all = group_all[:, G * NS :].reshape(tok_rows, G, NS)
    write_here = lax.dynamic_slice_in_dim(write_all, first_group, groups_here, 1)
    read_here = lax.dynamic_slice_in_dim(read_all, first_group, groups_here, 1)
    step_size = jax.nn.softplus(dt_proj.astype(jnp.float32) + dt_bias)
    decay_rate = step_size * jnp.exp(a_log)
    cumulative = jnp.cumsum(decay_rate, 0)
    block_end = cumulative[-1]
    causal = lax.broadcasted_iota(jnp.int32, (tok_rows, tok_rows), 0) >= lax.broadcasted_iota(
        jnp.int32, (tok_rows, tok_rows), 1
    )
    spread = cumulative.T[:, :, None] - cumulative.T[:, None, :]
    decay_mask = jnp.where(causal, jnp.exp(-jnp.where(causal, spread, 0.0)), 0.0)
    scores = jnp.einsum("tgn,sgn->gts", read_here, write_here, preferred_element_type=jnp.float32)
    weights = (
        scores[:, None]
        * decay_mask.reshape(groups_here, heads_local, tok_rows, tok_rows)
        * step_size.T.reshape(groups_here, heads_local, 1, tok_rows)
    ).astype(jnp.bfloat16)
    x_heads = x_conv.reshape(tok_rows, groups_here, heads_local, head_size)
    within_block = jnp.einsum(
        "ghts,sghp->tghp", weights, x_heads, preferred_element_type=jnp.float32
    )
    update = (
        (jnp.exp(-(block_end - cumulative)) * step_size).reshape(
            tok_rows, groups_here, heads_local
        )[..., None]
        * x_heads
    ).astype(jnp.bfloat16)
    contrib = jnp.einsum("sghp,sgn->ghpn", update, write_here, preferred_element_type=jnp.float32)
    identity = (jnp.ones((groups_here, heads_local), jnp.float32), jnp.zeros_like(contrib))
    carried = entering(
        (jnp.exp(-block_end).reshape(groups_here, heads_local), contrib),
        "ctx",
        chain_states,
        identity,
    )
    from_before = jnp.exp(-cumulative).reshape(tok_rows, groups_here, heads_local)[
        ..., None
    ] * jnp.einsum("tgn,ghpn->tghp", read_here.astype(jnp.float32), carried[1], precision=HIGH)
    output_raw = (
        within_block
        + from_before
        + d_skip.reshape(groups_here, heads_local)[None, :, :, None] * x_heads.astype(jnp.float32)
    )
    mean_square = jnp.mean(output_raw * output_raw, -1, keepdims=True)
    normed = (
        output_raw
        * lax.rsqrt(mean_square + 1e-05)
        * norm_gain.reshape(groups_here, heads_local, head_size)
    )
    return (normed.reshape(1, tok_rows, x_cols).astype(jnp.bfloat16), kurtosis)


def hadamard(order):
    return hadamard_signs(order)


def rotated_half(tokens, which):
    rows, width = tokens.shape
    lanes = 256
    tiles = width // lanes
    first = jnp.einsum(
        "tab,bd->tad",
        tokens.reshape(rows, tiles, lanes),
        hadamard(lanes).astype(jnp.bfloat16),
        preferred_element_type=jnp.float32,
    )
    sign = 1.0 - 2.0 * which.astype(jnp.float32)
    kept = first[:, : tiles // 2] + sign * first[:, tiles // 2 :]
    span = tiles // 4
    while span:
        pairs = kept.reshape(rows, tiles // 4 // span, 2, span, lanes)
        kept = jnp.stack([pairs[:, :, 0] + pairs[:, :, 1], pairs[:, :, 0] - pairs[:, :, 1]], 2)
        span //= 2
    return (kept.reshape(rows, width // 2) / (width**0.5)).astype(jnp.bfloat16)


def swapped(value):
    return lax.ppermute(value, "mp", [(0, 1), (1, 0)])


def own_bc(array, me):
    half = array.shape[1] // 2
    keep = lax.dynamic_slice_in_dim(array, me * half, half, 1)
    give = lax.dynamic_slice_in_dim(array, (1 - me) * half, half, 1)
    got = swapped(give)
    return jnp.where(me == 0, keep, got), jnp.where(me == 0, got, keep)


def own_cut(array, place, count, axis):
    size = array.shape[axis] // count
    return lax.dynamic_slice_in_dim(array, place * size, size, axis)


ROWS = ("dp", "ctx")


def shards_by_heads(
    tokens, x_weight, bc_weight, dt_weight, conv_x, conv_bc, dt_bias, a_log, d_skip, norm_gain
):
    me = lax.axis_index("mp")
    place = lax.axis_index(ROWS)
    count = lax.axis_size(ROWS)
    seqs, blks = lax.axis_size("dp"), lax.axis_size("ctx")
    tok_rows, width = tokens.shape[1:]
    all_rows = count * tok_rows
    depth = x_weight.shape[0]
    heads = dt_weight.shape[1] // count
    groups_here = dt_weight.shape[1] // (HEADS // G)
    per_group = count // groups_here
    bc_cols = groups_here * NS // count
    x_cols = x_weight.shape[1] // count
    head_size = x_cols // heads

    write_w, read_w = own_bc(bc_weight, me)
    pieces = jnp.concatenate(
        [
            x_weight.reshape(depth, count, x_cols),
            write_w.reshape(depth, count, bc_cols),
            read_w.reshape(depth, count, bc_cols),
            dt_weight.reshape(depth, count, heads),
        ],
        2,
    )
    panel = lax.all_to_all(pieces, ROWS, 1, 0, tiled=True).reshape(width, -1)
    half = width // 2
    panel_keep = lax.dynamic_slice_in_dim(panel, me * half, half, 0)
    panel_got = swapped(lax.dynamic_slice_in_dim(panel, (1 - me) * half, half, 0))

    rotated = lax.all_gather(rotated_half(tokens[0], me), ROWS, axis=0, tiled=True)
    wide = rotated.astype(jnp.float32)
    square = wide * wide
    powers = [
        jnp.sum(wide, 0),
        jnp.sum(square, 0),
        jnp.sum(square * wide, 0),
        jnp.sum(square * square, 0),
    ]
    kurtosis = kurtosis_from(powers, float(all_rows))

    theirs = jnp.dot(rotated, panel_got, preferred_element_type=jnp.float32)
    mine = jnp.dot(rotated, panel_keep, preferred_element_type=jnp.float32)
    joined = (mine + swapped(theirs)).astype(jnp.bfloat16)

    write_t, read_t = own_bc(conv_bc, me)
    taps = jnp.concatenate(
        [own_cut(conv_x, place, count, 1), own_cut(write_t, place, count, 1), own_cut(read_t, place, count, 1)], 1
    )
    kernel = taps.shape[0] - 1
    seq_len = blks * tok_rows
    chans = taps.shape[1]
    padded = jnp.pad(joined[:, :chans].reshape(seqs, seq_len, chans), ((0, 0), (kernel - 1, 0), (0, 0)))
    conv_sum = taps[kernel]
    for tap_index in range(kernel):
        conv_sum = conv_sum + taps[tap_index] * padded[:, tap_index : tap_index + seq_len]
    convolved = jax.nn.silu(conv_sum).astype(jnp.bfloat16)
    members = [[g * per_group + i for i in range(per_group)] for g in range(groups_here)]
    bc = lax.all_gather(
        convolved[:, :, x_cols:].reshape(all_rows, 2 * bc_cols), ROWS, axis=0, axis_index_groups=members
    )
    bc = bc.reshape(per_group, seqs, blks, tok_rows, 2, bc_cols).transpose(4, 1, 2, 3, 0, 5)
    write, read = bc.reshape(2, seqs, blks, tok_rows, NS)
    x_heads = convolved[:, :, :x_cols].reshape(seqs, blks, tok_rows, heads, head_size)

    dt = lax.optimization_barrier(joined[:, chans:]).astype(jnp.float32)
    step = jax.nn.softplus(dt + own_cut(dt_bias, place, count, 0))
    rate = (step * jnp.exp(own_cut(a_log, place, count, 0))).reshape(seqs, blks, tok_rows, heads)
    step = step.reshape(seqs, blks, tok_rows, heads)
    cum = jnp.cumsum(rate, 2)
    end = cum[:, :, -1]
    causal = lax.broadcasted_iota(jnp.int32, (tok_rows, tok_rows), 0) >= lax.broadcasted_iota(
        jnp.int32, (tok_rows, tok_rows), 1
    )
    cum_h = cum.transpose(0, 1, 3, 2)
    spread = cum_h[..., :, None] - cum_h[..., None, :]
    decay = jnp.where(causal, jnp.exp(-jnp.where(causal, spread, 0.0)), 0.0)
    scores = jnp.einsum("bktn,bksn->bkts", read, write, preferred_element_type=jnp.float32)
    weights = (
        scores[:, :, None] * decay * step.transpose(0, 1, 3, 2)[:, :, :, None, :]
    ).astype(jnp.bfloat16)
    within = jnp.einsum("bkhts,bkshp->bkthp", weights, x_heads, preferred_element_type=jnp.float32)
    update = (
        (jnp.exp(-(end[:, :, None] - cum)) * step)[..., None] * x_heads.astype(jnp.float32)
    ).astype(jnp.bfloat16)
    contrib = jnp.einsum("bkshp,bksn->bkhpn", update, write, preferred_element_type=jnp.float32)
    state = jnp.zeros_like(contrib[:, 0])
    states = []
    for blk in range(blks):
        states.append(state)
        state = jnp.exp(-end[:, blk])[..., None, None] * state + contrib[:, blk]
    carried = jnp.stack(states, 1)
    read_wide = read.astype(jnp.float32)
    before = jnp.exp(-cum)[..., None] * jnp.einsum(
        "bktn,bkhpn->bkthp", read_wide, carried, preferred_element_type=jnp.float32
    )
    raw = within + before + own_cut(d_skip, place, count, 0)[:, None] * x_heads.astype(jnp.float32)
    gain = own_cut(norm_gain, place, count, 0).reshape(heads, head_size)
    out = (raw * lax.rsqrt(jnp.mean(raw * raw, -1, keepdims=True) + 1e-05) * gain).astype(jnp.bfloat16)
    out = out.reshape(count, tok_rows, x_cols)
    out = lax.all_to_all(out, ROWS, 0, 2, tiled=True)
    return out, kurtosis


def shards(tokens, x_weight, bc_weight, dt_weight, *rest):
    count = lax.axis_size(ROWS)
    heads_dev = dt_weight.shape[1]
    groups_here = heads_dev // (HEADS // G)
    by_heads = (
        lax.axis_size("mp") == 2
        and heads_dev % count == 0
        and groups_here > 0
        and count % groups_here == 0
        and tokens.shape[0] == 1
    )
    plan = shards_by_heads if by_heads else shards_by_rows
    return plan(tokens, x_weight, bc_weight, dt_weight, *rest)


def solution(mesh):
    return jax.shard_map(
        shards,
        mesh=mesh,
        in_specs=(
            P("dp", "ctx", None),
            P(("dp", "ctx"), "mp"),
            P(("dp", "ctx"), "mp"),
            P(("dp", "ctx"), "mp"),
            P(None, "mp"),
            P(None, "mp"),
            P("mp"),
            P("mp"),
            P("mp"),
            P("mp"),
        ),
        out_specs=(P("dp", "ctx", "mp"), P("mp")),
        check_vma=False,
    )
```

```python
import jax
import jax.numpy as jnp
from jax import lax
from jax.experimental import pallas as pl
from jax.experimental.pallas import tpu as pltpu
from jax.sharding import PartitionSpec as P

ROOT = 64
HEADS = 128
G = 4
NS = 128


HIGH = lax.Precision.HIGHEST


def passed_along(value, axis, steps):
    count = lax.axis_size(axis)
    first, last = (max(0, -steps), min(count, count - steps))
    return lax.ppermute(value, axis, [(source, source + steps) for source in range(first, last)])


def entering(array, axis, combine, identity):
    length, place = (lax.axis_size(axis), lax.axis_index(axis))
    everything = jax.tree.map(
        lambda part, kind: lax.all_gather(part.astype(kind), axis),
        array,
        (jnp.bfloat16, jnp.bfloat16),
    )
    start = jax.tree.map(
        lambda part, zero: jnp.broadcast_to(jnp.asarray(zero, part.dtype), part.shape),
        array,
        identity,
    )

    def step(k, before):
        reached = k < place
        new = combine(
            before, jax.tree.map(lambda part, own: part[k].astype(own.dtype), everything, array)
        )
        return jax.tree.map(lambda a, b: jnp.where(reached, a, b), new, before)

    return lax.fori_loop(0, length, step, start)


def hadamard_signs(sign_order):
    row_index = lax.broadcasted_iota(jnp.int32, (sign_order, sign_order), 0)
    col_index = lax.broadcasted_iota(jnp.int32, (sign_order, sign_order), 1)
    common = jnp.bitwise_and(row_index, col_index)
    parity = jnp.zeros((sign_order, sign_order), jnp.int32)
    for bit_index in range(sign_order.bit_length() - 1):
        parity = parity + jnp.bitwise_and(jnp.right_shift(common, bit_index), 1)
    return 1.0 - 2.0 * jnp.bitwise_and(parity, 1).astype(jnp.float32)


def kurtosis_from(powers, row_count):
    average = powers[0] / row_count
    second = powers[1] / row_count - average * average
    fourth = (
        powers[3] / row_count
        - 4.0 * average * powers[2] / row_count
        + 6.0 * average * average * powers[1] / row_count
        - 3.0 * average * average * average * average
    )
    return fourth / (second * second + 1e-06)


def chain_states(earlier, later):
    return (earlier[0] * later[0], later[0][:, :, None, None] * earlier[1] + later[1])


def shards_by_rows(
    tokens, x_weight, bc_weight, dt_weight, conv_x, conv_bc, dt_bias, a_log, d_skip, norm_gain
):
    tok_rows = tokens.shape[1]
    model_width = tokens.shape[2]
    signs = hadamard_signs(ROOT)
    blocks = tokens.reshape(tok_rows, ROOT, ROOT)
    first_pass = jnp.einsum(
        "tab,ac->tcb", blocks, signs.astype(jnp.bfloat16), preferred_element_type=jnp.float32
    )
    second = jnp.einsum("tcb,bd->tcd", first_pass, signs, precision=HIGH)
    rotated = (second.reshape(tok_rows, model_width) / ROOT).astype(jnp.bfloat16)
    channel_share = model_width // lax.axis_size("mp")
    own_cols = lax.dynamic_slice_in_dim(
        rotated, lax.axis_index("mp") * channel_share, channel_share, 1
    ).astype(jnp.float32)
    square = own_cols * own_cols
    powers = jnp.stack(
        [
            jnp.sum(own_cols, 0),
            jnp.sum(square, 0),
            jnp.sum(square * own_cols, 0),
            jnp.sum(square * square, 0),
        ]
    )
    row_count = float(tok_rows * lax.axis_size("dp") * lax.axis_size("ctx"))
    totals = lax.psum(powers, ("dp", "ctx"))
    kurtosis = kurtosis_from(totals, row_count)
    panels = (
        lax.all_gather(x_weight, ("dp", "ctx"), axis=0, tiled=True),
        lax.all_gather(bc_weight, ("dp", "ctx"), axis=0, tiled=True),
        lax.all_gather(dt_weight, ("dp", "ctx"), axis=0, tiled=True),
    )
    projected = tuple(
        (jnp.dot(rotated, panel, preferred_element_type=jnp.float32) for panel in panels)
    )
    x_cols = x_weight.shape[1]
    joined = jnp.concatenate(
        [projected[0].astype(jnp.bfloat16), projected[1].astype(jnp.bfloat16)], 1
    )
    dt_proj = lax.optimization_barrier(projected[2].astype(jnp.bfloat16))
    conv_taps = jnp.concatenate([conv_x, conv_bc], 1)
    kernel = conv_taps.shape[0] - 1
    rim_rows = passed_along(joined[tok_rows - (kernel - 1) :], "ctx", 1)
    padded = jnp.concatenate([rim_rows, joined], 0)
    conv_sum = conv_taps[kernel]
    for tap_index in range(kernel):
        conv_sum = conv_sum + conv_taps[tap_index] * padded[tap_index : tap_index + tok_rows]
    convolved = jax.nn.silu(conv_sum).astype(jnp.bfloat16)
    x_conv = convolved[:, :x_cols]
    group_all = lax.all_gather(convolved[:, x_cols:], "mp", axis=1, tiled=True)
    heads_dev = dt_weight.shape[1]
    head_size = x_cols // heads_dev
    per_group = HEADS // G
    groups_here = max(1, heads_dev // per_group)
    heads_local = heads_dev // groups_here
    first_group = lax.axis_index("mp") * heads_dev // per_group
    write_all = group_all[:, : G * NS].reshape(tok_rows, G, NS)
    read_all = group_all[:, G * NS :].reshape(tok_rows, G, NS)
    write_here = lax.dynamic_slice_in_dim(write_all, first_group, groups_here, 1)
    read_here = lax.dynamic_slice_in_dim(read_all, first_group, groups_here, 1)
    step_size = jax.nn.softplus(dt_proj.astype(jnp.float32) + dt_bias)
    decay_rate = step_size * jnp.exp(a_log)
    cumulative = jnp.cumsum(decay_rate, 0)
    block_end = cumulative[-1]
    causal = lax.broadcasted_iota(jnp.int32, (tok_rows, tok_rows), 0) >= lax.broadcasted_iota(
        jnp.int32, (tok_rows, tok_rows), 1
    )
    spread = cumulative.T[:, :, None] - cumulative.T[:, None, :]
    decay_mask = jnp.where(causal, jnp.exp(-jnp.where(causal, spread, 0.0)), 0.0)
    scores = jnp.einsum("tgn,sgn->gts", read_here, write_here, preferred_element_type=jnp.float32)
    weights = (
        scores[:, None]
        * decay_mask.reshape(groups_here, heads_local, tok_rows, tok_rows)
        * step_size.T.reshape(groups_here, heads_local, 1, tok_rows)
    ).astype(jnp.bfloat16)
    x_heads = x_conv.reshape(tok_rows, groups_here, heads_local, head_size)
    within_block = jnp.einsum(
        "ghts,sghp->tghp", weights, x_heads, preferred_element_type=jnp.float32
    )
    update = (
        (jnp.exp(-(block_end - cumulative)) * step_size).reshape(
            tok_rows, groups_here, heads_local
        )[..., None]
        * x_heads
    ).astype(jnp.bfloat16)
    contrib = jnp.einsum("sghp,sgn->ghpn", update, write_here, preferred_element_type=jnp.float32)
    identity = (jnp.ones((groups_here, heads_local), jnp.float32), jnp.zeros_like(contrib))
    carried = entering(
        (jnp.exp(-block_end).reshape(groups_here, heads_local), contrib),
        "ctx",
        chain_states,
        identity,
    )
    from_before = jnp.exp(-cumulative).reshape(tok_rows, groups_here, heads_local)[
        ..., None
    ] * jnp.einsum("tgn,ghpn->tghp", read_here.astype(jnp.float32), carried[1], precision=HIGH)
    output_raw = (
        within_block
        + from_before
        + d_skip.reshape(groups_here, heads_local)[None, :, :, None] * x_heads.astype(jnp.float32)
    )
    mean_square = jnp.mean(output_raw * output_raw, -1, keepdims=True)
    normed = (
        output_raw
        * lax.rsqrt(mean_square + 1e-05)
        * norm_gain.reshape(groups_here, heads_local, head_size)
    )
    return (normed.reshape(1, tok_rows, x_cols).astype(jnp.bfloat16), kurtosis)


def hadamard(order):
    return hadamard_signs(order)


def rotated_half(tokens, which):
    rows, width = tokens.shape
    lanes = 256
    tiles = width // lanes
    first = jnp.einsum(
        "tab,bd->tad",
        tokens.reshape(rows, tiles, lanes),
        hadamard(lanes).astype(jnp.bfloat16),
        preferred_element_type=jnp.float32,
    )
    sign = 1.0 - 2.0 * which.astype(jnp.float32)
    kept = first[:, : tiles // 2] + sign * first[:, tiles // 2 :]
    span = tiles // 4
    while span:
        pairs = kept.reshape(rows, tiles // 4 // span, 2, span, lanes)
        kept = jnp.stack([pairs[:, :, 0] + pairs[:, :, 1], pairs[:, :, 0] - pairs[:, :, 1]], 2)
        span //= 2
    return (kept.reshape(rows, width // 2) / (width**0.5)).astype(jnp.bfloat16)


def swapped(value):
    return lax.ppermute(value, "mp", [(0, 1), (1, 0)])


def own_bc(array, me):
    half = array.shape[1] // 2
    keep = lax.dynamic_slice_in_dim(array, me * half, half, 1)
    give = lax.dynamic_slice_in_dim(array, (1 - me) * half, half, 1)
    got = swapped(give)
    return jnp.where(me == 0, keep, got), jnp.where(me == 0, got, keep)


def own_cut(array, place, count, axis):
    size = array.shape[axis] // count
    return lax.dynamic_slice_in_dim(array, place * size, size, axis)


ROWS = ("dp", "ctx")


MESH = pl.DeviceIdType.MESH


def greet(peers):
    barrier = pltpu.get_barrier_semaphore()
    for peer in peers:
        pl.semaphore_signal(barrier, inc=1, device_id=peer, device_id_type=MESH)
    pl.semaphore_wait(barrier, len(peers))


def sent(source, target, send_sem, recv_sem, peer):
    copy = pltpu.make_async_remote_copy(
        src_ref=source,
        dst_ref=target,
        send_sem=send_sem,
        recv_sem=recv_sem,
        device_id=peer,
        device_id_type=MESH,
    )
    copy.start()
    return copy


def spread_kernel(
    rot_ref, piece_ref, all_ref, panel_ref,
    own_sem, line_send, line_recv, side_send, side_recv, diag_send, diag_recv, part_send, part_recv,
):
    dp, ctx, me = lax.axis_index("dp"), lax.axis_index("ctx"), lax.axis_index("mp")
    blks = lax.axis_size("ctx")
    count = 4 * blks
    place = dp * blks + ctx
    by_x = dp + 1 - 2 * lax.rem(dp, 2)
    by_y = lax.rem(dp + 2, 4)

    def peer_of(step):
        other = lax.rem(place + step, count)
        return other, (other // blks, lax.rem(other, blks), me)

    greet([peer_of(step)[1] for step in range(1, count)])
    own = [
        pltpu.make_async_copy(rot_ref, all_ref.at[place], own_sem.at[0]),
        pltpu.make_async_copy(piece_ref.at[place], panel_ref.at[place], own_sem.at[1]),
    ]
    line, side, diag = [], [], []

    def to_sides(step, source, index):
        for way, corner in ((0, by_x), (1, by_y)):
            side.append(
                sent(
                    source, all_ref.at[index], side_send.at[step, way], side_recv.at[step, way],
                    (corner, ctx, me),
                )
            )

    for step in range(1, blks):
        to = (dp, lax.rem(ctx + step, blks), me)
        line.append(
            sent(rot_ref, all_ref.at[place], line_send.at[step], line_recv.at[step], to)
        )
    to_sides(0, rot_ref, place)
    for copy in own:
        copy.start()
    parts = []
    for step in range(1, count):
        other, to = peer_of(step)
        parts.append(
            sent(
                piece_ref.at[other], panel_ref.at[place], part_send.at[step], part_recv.at[step], to
            )
        )

    half = rot_ref.shape[0] // 2
    for step in range(blks):
        source_ctx = lax.rem(ctx - step + blks, blks)
        if step:
            line[step - 1].wait_recv()
            index = dp * blks + source_ctx
            to_sides(step, all_ref.at[index], index)
    for step in range(blks):
        source_ctx = lax.rem(ctx - step + blks, blks)
        for way, corner, onward in ((0, by_x, by_y), (1, by_y, by_x)):
            side[2 * step + way].wait_recv()
            part = all_ref.at[corner * blks + source_ctx, pl.ds(way * half, half)]
            diag.append(
                sent(
                    part, part, diag_send.at[step, way], diag_recv.at[step, way],
                    (onward, ctx, me),
                )
            )
    for copy in diag + parts:
        copy.wait_recv()
    for copy in line + side + diag + parts:
        copy.wait_send()
    for copy in own:
        copy.wait()


def exchange_blocks(rotated, pieces, blks):
    count = 4 * blks
    dma = pltpu.SemaphoreType.DMA
    anywhere = pl.BlockSpec(memory_space=pl.ANY)
    return pl.pallas_call(
        spread_kernel,
        out_shape=(
            jax.ShapeDtypeStruct((count,) + rotated.shape, rotated.dtype),
            jax.ShapeDtypeStruct(pieces.shape, pieces.dtype),
        ),
        in_specs=[anywhere] * 2,
        out_specs=(anywhere, anywhere),
        scratch_shapes=[
            dma((2,)), dma((blks,)), dma((blks,)), dma((blks, 2)), dma((blks, 2)),
            dma((blks, 2)), dma((blks, 2)), dma((count,)), dma((count,)),
        ],
        compiler_params=pltpu.CompilerParams(collective_id=0, has_side_effects=True),
    )(rotated, pieces)


def group_kernel(members, own_ref, all_ref, own_sem, send, recv):
    dp, ctx, me = lax.axis_index("dp"), lax.axis_index("ctx"), lax.axis_index("mp")
    blks = lax.axis_size("ctx")
    place = dp * blks + ctx
    first = place // members * members
    seat = place - first
    peers = []
    for step in range(1, members):
        other = first + lax.rem(seat + step, members)
        peers.append((other // blks, lax.rem(other, blks), me))
    greet(peers)
    own = pltpu.make_async_copy(own_ref, all_ref.at[seat], own_sem)
    own.start()
    copies = [
        sent(own_ref, all_ref.at[seat], send.at[step], recv.at[step], peer)
        for step, peer in enumerate(peers)
    ]
    for copy in copies:
        copy.wait_recv()
    for copy in copies:
        copy.wait_send()
    own.wait()


def group_gather(own, members):
    dma = pltpu.SemaphoreType.DMA
    anywhere = pl.BlockSpec(memory_space=pl.ANY)
    return pl.pallas_call(
        lambda *refs: group_kernel(members, *refs),
        out_shape=jax.ShapeDtypeStruct((members,) + own.shape, own.dtype),
        in_specs=[anywhere],
        out_specs=anywhere,
        scratch_shapes=[dma, dma((members - 1,)), dma((members - 1,))],
        compiler_params=pltpu.CompilerParams(collective_id=1, has_side_effects=True),
    )(own)


def shards_by_heads(
    tokens, x_weight, bc_weight, dt_weight, conv_x, conv_bc, dt_bias, a_log, d_skip, norm_gain
):
    me = lax.axis_index("mp")
    place = lax.axis_index(ROWS)
    count = lax.axis_size(ROWS)
    seqs, blks = lax.axis_size("dp"), lax.axis_size("ctx")
    tok_rows, width = tokens.shape[1:]
    all_rows = count * tok_rows
    depth = x_weight.shape[0]
    heads = dt_weight.shape[1] // count
    groups_here = dt_weight.shape[1] // (HEADS // G)
    per_group = count // groups_here
    bc_cols = groups_here * NS // count
    x_cols = x_weight.shape[1] // count
    head_size = x_cols // heads

    write_w, read_w = own_bc(bc_weight, me)
    small = jnp.concatenate(
        [
            write_w.reshape(depth, count, bc_cols),
            read_w.reshape(depth, count, bc_cols),
            dt_weight.reshape(depth, count, heads),
        ],
        2,
    )
    small_cols = small.shape[2]
    folds = 4
    lanes = x_cols // folds
    small = jnp.pad(small, ((0, 0), (0, 0), (0, lanes - small_cols)))
    small = small.reshape(folds, depth // folds, count, lanes).transpose(2, 1, 0, 3)
    pieces = jnp.concatenate(
        [
            x_weight.reshape(depth, count, x_cols).transpose(1, 0, 2),
            small.reshape(count, depth // folds, x_cols),
        ],
        1,
    )
    rotated, panels = exchange_blocks(rotated_half(tokens[0], me), pieces, blks)
    rotated = rotated.reshape(all_rows, width // 2)
    small = panels[:, depth:].reshape(count, depth // folds, folds, lanes).transpose(0, 2, 1, 3)
    panel = jnp.concatenate(
        [panels[:, :depth].reshape(width, x_cols), small.reshape(width, lanes)[:, :small_cols]], 1
    )
    half = width // 2
    panel_keep = lax.dynamic_slice_in_dim(panel, me * half, half, 0)
    panel_got = swapped(lax.dynamic_slice_in_dim(panel, (1 - me) * half, half, 0))

    wide = rotated.astype(jnp.float32)
    square = wide * wide
    powers = [
        jnp.sum(wide, 0),
        jnp.sum(square, 0),
        jnp.sum(square * wide, 0),
        jnp.sum(square * square, 0),
    ]
    kurtosis = kurtosis_from(powers, float(all_rows))

    theirs = jnp.dot(rotated, panel_got, preferred_element_type=jnp.float32)
    mine = jnp.dot(rotated, panel_keep, preferred_element_type=jnp.float32)
    joined = (mine + swapped(theirs)).astype(jnp.bfloat16)

    write_t, read_t = own_bc(conv_bc, me)
    taps = jnp.concatenate(
        [own_cut(conv_x, place, count, 1), own_cut(write_t, place, count, 1), own_cut(read_t, place, count, 1)], 1
    )
    kernel = taps.shape[0] - 1
    seq_len = blks * tok_rows
    chans = taps.shape[1]
    padded = jnp.pad(joined[:, :chans].reshape(seqs, seq_len, chans), ((0, 0), (kernel - 1, 0), (0, 0)))
    conv_sum = taps[kernel]
    for tap_index in range(kernel):
        conv_sum = conv_sum + taps[tap_index] * padded[:, tap_index : tap_index + seq_len]
    convolved = jax.nn.silu(conv_sum).astype(jnp.bfloat16)
    bc = convolved[:, :, x_cols:].transpose(1, 0, 2).reshape(seq_len, seqs * 2 * bc_cols)
    bc = group_gather(bc, per_group).reshape(per_group, blks, tok_rows, seqs, 2, bc_cols)
    bc = bc.transpose(4, 3, 1, 2, 0, 5)
    write, read = bc.reshape(2, seqs, blks, tok_rows, NS)
    x_heads = convolved[:, :, :x_cols].reshape(seqs, blks, tok_rows, heads, head_size)

    dt = lax.optimization_barrier(joined[:, chans:]).astype(jnp.float32)
    step = jax.nn.softplus(dt + own_cut(dt_bias, place, count, 0))
    rate = (step * jnp.exp(own_cut(a_log, place, count, 0))).reshape(seqs, blks, tok_rows, heads)
    step = step.reshape(seqs, blks, tok_rows, heads)
    causal = lax.broadcasted_iota(jnp.int32, (tok_rows, tok_rows), 0) >= lax.broadcasted_iota(
        jnp.int32, (tok_rows, tok_rows), 1
    )
    cum = jnp.einsum("ts,bksh->bkth", causal.astype(jnp.float32), rate, precision=HIGH)
    end = cum[:, :, -1]
    cum_h = cum.transpose(0, 1, 3, 2)
    spread = cum_h[..., :, None] - cum_h[..., None, :]
    decay = jnp.where(causal, jnp.exp(-jnp.where(causal, spread, 0.0)), 0.0)
    scores = jnp.einsum("bktn,bksn->bkts", read, write, preferred_element_type=jnp.float32)
    weights = (
        scores[:, :, None] * decay * step.transpose(0, 1, 3, 2)[:, :, :, None, :]
    ).astype(jnp.bfloat16)
    within = jnp.einsum("bkhts,bkshp->bkthp", weights, x_heads, preferred_element_type=jnp.float32)
    update = (
        (jnp.exp(-(end[:, :, None] - cum)) * step)[..., None] * x_heads.astype(jnp.float32)
    ).astype(jnp.bfloat16)
    contrib = jnp.einsum("bkshp,bksn->bkhpn", update, write, preferred_element_type=jnp.float32)
    state = jnp.zeros_like(contrib[:, 0])
    states = []
    for blk in range(blks):
        states.append(state)
        state = jnp.exp(-end[:, blk])[..., None, None] * state + contrib[:, blk]
    carried = jnp.stack(states, 1)
    read_wide = read.astype(jnp.float32)
    before = jnp.exp(-cum)[..., None] * jnp.einsum(
        "bktn,bkhpn->bkthp", read_wide, carried, preferred_element_type=jnp.float32
    )
    raw = within + before + own_cut(d_skip, place, count, 0)[:, None] * x_heads.astype(jnp.float32)
    gain = own_cut(norm_gain, place, count, 0).reshape(heads, head_size)
    out = (raw * lax.rsqrt(jnp.mean(raw * raw, -1, keepdims=True) + 1e-05) * gain).astype(jnp.bfloat16)
    out = out.reshape(count, tok_rows, x_cols)
    out = lax.all_to_all(out, ROWS, 0, 2, tiled=True)
    return out, kurtosis


def shards(tokens, x_weight, bc_weight, dt_weight, *rest):
    count = lax.axis_size(ROWS)
    heads_dev = dt_weight.shape[1]
    groups_here = heads_dev // (HEADS // G)
    by_heads = (
        lax.axis_size("mp") == 2
        and heads_dev % count == 0
        and groups_here > 0
        and count % groups_here == 0
        and tokens.shape[0] == 1
        and lax.axis_size("dp") == 4
    )
    plan = shards_by_heads if by_heads else shards_by_rows
    return plan(tokens, x_weight, bc_weight, dt_weight, *rest)


def solution(mesh):
    return jax.shard_map(
        shards,
        mesh=mesh,
        in_specs=(
            P("dp", "ctx", None),
            P(("dp", "ctx"), "mp"),
            P(("dp", "ctx"), "mp"),
            P(("dp", "ctx"), "mp"),
            P(None, "mp"),
            P(None, "mp"),
            P("mp"),
            P("mp"),
            P("mp"),
            P("mp"),
        ),
        out_specs=(P("dp", "ctx", "mp"), P("mp")),
        check_vma=False,
    )
```
